32 devices in a mesh: pix: 4 (over y, x), act: 8 (over z, core).
Axes of the slice: x: 2, y: 2, z: 4, core: 2. Of those that a mesh axis runs over, the one named last changes fastest.
Arguments:
- jacobian: bfloat16 [1024, 18432], P('pix', 'act'), may hold values from -0.1875 to 0.1875
- dark_field: float32 [1024], P('pix'), may hold values from -6 to 6
- update: float32 [18432], P('act'), may hold values from -3 to 3
- pixel_mask: int32 [1024], P('pix'), may hold values 0 or 1
- act_mask: int32 [18432], P('act'), may hold values 0 or 1
Outputs:
- gram_matrix: float32 [18432, 18432], P('act', 'pix')
- projected: float32 [18432], P('act')
- predicted: float32 [1024], P('pix')
The draws below stay inside these ranges and needn't reach their ends.
All inputs are finite; a program needn't handle non-finite values. No bound on the sum of `pixel_mask` or of `act_mask` on one device may be relied on, other than what follows from the above.
Results may differ from the reference program's by a relative error of at most 0.0003.
Values may be sent and summed in bfloat16 or wider, within the bound.
A program may use at most 128 MiB of HBM per device.

```python
import jax
import jax.numpy as jnp
from jax import lax

NACT = 18432
ROWS = 1024


def plant(entries, key, smallest, largest):
    spot = [jax.random.randint(jax.random.fold_in(key, axis), (), 0, length) for axis, length in enumerate(entries.shape)]
    longest = entries.shape.index(max(entries.shape))
    neighbour = spot[:longest] + [(spot[longest] + 1) % entries.shape[longest]] + spot[longest + 1:]
    return entries.at[tuple(spot)].set(smallest).at[tuple(neighbour)].set(largest)


def block_levels(rng, dims, split, low, high):
    def one(dim, shards_of):
        draws = jax.random.uniform(jax.random.fold_in(jax.random.fold_in(rng, 6), dim), (shards_of,), jnp.float32, low / len(split), high / len(split))
        return jnp.repeat(jnp.exp(draws), dims[dim] // shards_of).reshape((-1,) + (1,) * (len(dims) - dim - 1))

    factor_of = one(*split[0])
    for cut in split[1:]:
        factor_of = factor_of * one(*cut)
    return factor_of


def noise(own_key, extent, width, most, pieces=(), held_as=jnp.bfloat16):
    drawn = width * jax.random.normal(own_key, extent, jnp.float32)
    if pieces:
        drawn = drawn * block_levels(own_key, extent, pieces, -0.22, 0.18)
    return jnp.clip(drawn, -most, most).astype(held_as)


def setup_inputs(seed: int = 0) -> dict:
    key_list = jax.random.split(jax.random.key(seed), 6)
    return {
        "jacobian": noise(key_list[0], (ROWS, NACT), ROWS ** -0.5, 0.1875, ((0, 4), (1, 8))),
        "dark_field": noise(key_list[1], (ROWS,), 1.0, 6.0, ((0, 4),), jnp.float32),
        "update": noise(key_list[2], (NACT,), 0.5, 3.0, ((0, 8),), jnp.float32),
        "pixel_mask": plant((jax.random.randint(key_list[3], (ROWS,), 0, 4) < 3).astype(jnp.int32), jax.random.fold_in(key_list[3], 1), 0, 1),
        "act_mask": plant((jax.random.randint(key_list[4], (NACT,), 0, 8) < 7).astype(jnp.int32), jax.random.fold_in(key_list[4], 1), 0, 1),
    }


def reference(jacobian, dark_field, update, pixel_mask, act_mask):
    keep = (pixel_mask[:, None] * act_mask[None, :]) > 0
    masked_jac = jnp.where(keep, jacobian, jnp.zeros_like(jacobian))
    gram_matrix = lax.dot_general(masked_jac, masked_jac, (((0,), (0,)), ((), ())), preferred_element_type=jnp.float32)
    weighted = pixel_mask.astype(jnp.float32) * dark_field
    projected = jnp.dot(weighted, masked_jac.astype(jnp.float32), precision=lax.Precision.HIGHEST, preferred_element_type=jnp.float32)
    strokes = act_mask.astype(jnp.float32) * update
    predicted = jnp.dot(masked_jac.astype(jnp.float32), strokes, precision=lax.Precision.HIGHEST, preferred_element_type=jnp.float32)
    return gram_matrix, projected, predicted
```

```python
import functools

import jax
import jax.numpy as jnp
from jax import lax
from jax.experimental import pallas as pl
from jax.experimental.pallas import tpu as pltpu
from jax.sharding import PartitionSpec as P

MESH = pl.DeviceIdType.MESH
F32 = jnp.float32
BF16 = jnp.bfloat16


def mixed(index, step, size):
    bit, out = 1, index
    while bit < size:
        if step & bit:
            out = out + bit - 2 * bit * ((index // bit) % 2)
        bit *= 2
    return out


def gather_kernel(
    npix, ngrp, chunks, via_line, jac, col, row, lhs, rhs, proj, pred,
    mj, relay, terms_f, terms_s, l_recv, r_recv, t_recv, s_recv, f_recv, p_recv, sends, local_sem,
):
    rows, cols = jac.shape
    ch = rows // chunks
    p = lax.axis_index("pix")
    a = lax.axis_index("act")
    z = a // 2
    c = a % 2
    root = p == z
    here = z >= 0
    nact = 2 * ngrp

    barrier = pltpu.get_barrier_semaphore()
    for d in range(1, npix):
        pl.semaphore_signal(barrier, inc=1, device_id={"pix": mixed(p, d, npix), "act": a}, device_id_type=MESH)
    for d in range(1, nact):
        pl.semaphore_signal(barrier, inc=1, device_id={"pix": p, "act": lax.rem(a + d, nact)}, device_id_type=MESH)

    def mask_step(i, carry):
        at = pl.ds(pl.multiple_of(i * 128, 128), 128)
        keep = col[:, 0:1] * row[0:1, at] > 0
        mj[:, at] = jnp.where(keep, jac[:, at].astype(F32), 0.0).astype(BF16)
        return carry

    lax.fori_loop(0, cols // 128, mask_step, 0)
    pl.semaphore_wait(barrier, npix - 1 + nact - 1)

    pending = []

    def send(cond, src, dst, rsem, pix, act):
        ssem = sends.at[len(pending)]

        def make():
            return pltpu.make_async_remote_copy(
                src_ref=src, dst_ref=dst, send_sem=ssem, recv_sem=rsem,
                device_id={"pix": pix, "act": act}, device_id_type=MESH,
            )

        @pl.when(cond)
        def _():
            make().start()

        pending.append((cond, make))

    def arrived(ref, sem):
        pltpu.make_async_copy(ref, ref, sem).wait()

    def at_rows(q, k):
        return pl.ds(pl.multiple_of(q * rows + k * ch, ch), ch)

    my_half = pl.ds(pl.multiple_of(c * cols, 128), cols)
    other_half = pl.ds(pl.multiple_of((1 - c) * cols, 128), cols)

    def l_ref(q, k):
        return lhs.at[at_rows(q, k), :]

    def r_ref(q, k):
        return rhs.at[at_rows(q, k), my_half]

    def own(k):
        return mj.at[pl.ds(k * ch, ch), :]

    up = z + 1 < ngrp
    down = z > 0

    def along_line(cond, src, q, k):
        send(cond & up & (z >= p), src, r_ref(q, k), r_recv.at[q, k], p, a + 2)
        send(cond & down & (z <= p), src, r_ref(q, k), r_recv.at[q, k], p, a - 2)

    def to_twin(cond, src, q, k):
        send(cond, src, r_ref(q, k), t_recv.at[q, k], p, 2 * z + 1 - c)

    for k in range(chunks):
        along_line(root, own(k), p, k)
        if k < via_line:
            send(jnp.logical_not(root) & up, own(k), relay.at[z, k], s_recv.at[z, k], p, a + 2)
            send(jnp.logical_not(root) & down, own(k), relay.at[z, k], s_recv.at[z, k], p, a - 2)
        for d in range(1, npix):
            send(here, own(k), l_ref(p, k), l_recv.at[p, k], mixed(p, d, npix), a)
    for k in range(chunks):
        to_twin(root, own(k), p, k)

    own_rows = pl.ds(pl.multiple_of(p * rows, rows), rows)
    keep_l = pltpu.make_async_copy(mj, lhs.at[own_rows, :], local_sem.at[0])
    keep_l.start()

    def term_step(i, acc):
        at = pl.ds(pl.multiple_of(i * 128, 128), 128)
        tile = mj[:, at].astype(F32)
        terms_f[p, :, at] = jnp.sum(tile * col[:, 1:2], axis=0, keepdims=True)
        return acc + tile * row[1:2, at]

    acc = lax.fori_loop(0, cols // 128, term_step, jnp.zeros((rows, 128), F32))
    terms_s[a] = jnp.sum(acc.T, axis=0, keepdims=True)
    for d in range(1, npix):
        send(here, terms_f.at[p], terms_f.at[p], f_recv.at[p], mixed(p, d, npix), a)
    for d in range(1, nact):
        send(here, terms_s.at[a], terms_s.at[a], p_recv.at[a], p, lax.rem(a + d, nact))

    events = []

    def on_l(d, k):
        def run():
            q = mixed(p, d, npix)
            arrived(l_ref(q, k), l_recv.at[q, k])
            if k >= via_line:
                along_line(root, l_ref(q, k), q, k)
            to_twin(root, l_ref(q, k), q, k)

        return run

    def on_s(dist, sign, k):
        def run():
            g = z - sign * dist
            there = (g >= 0) & (g < ngrp) & (g != p)
            slot = jnp.clip(g, 0, ngrp - 1)

            @pl.when(there)
            def _():
                arrived(relay.at[slot, k], s_recv.at[slot, k])

            if sign > 0:
                send(there & up, relay.at[slot, k], relay.at[slot, k], s_recv.at[slot, k], p, a + 2)
            else:
                send(there & down, relay.at[slot, k], relay.at[slot, k], s_recv.at[slot, k], p, a - 2)
            send(there, relay.at[slot, k], r_ref(p, k), r_recv.at[p, k], slot, a)

        return run

    def on_r(d, k):
        def run():
            q = mixed(p, d, npix)
            other = jnp.logical_not(root)

            @pl.when(other)
            def _():
                arrived(r_ref(q, k), r_recv.at[q, k])

            if d == 0 or k >= via_line:
                along_line(other, r_ref(q, k), q, k)
            to_twin(other, r_ref(q, k), q, k)

        return run

    unit = 4.0 / chunks
    for k in range(chunks):
        for d in range(1, npix):
            events.append((12 * unit * (k + 1) + 0.01 * d, on_l(d, k)))
        if k < via_line:
            for dist in range(1, ngrp):
                for sign in (1, -1):
                    events.append((6 * unit * (k + 1) + 18 * (dist - 1), on_s(dist, sign, k)))
        for d in range(npix):
            if d == 0:
                when = 6 * unit * (k + 1) + 12
            elif k >= via_line:
                when = 12 * unit * (k + 1) + 18
            else:
                when = 100 + k
            events.append((when, on_r(d, k)))
    events.sort(key=lambda e: e[0])
    for _, run in events:
        run()

    keep_l.wait()

    @pl.when(root)
    def _():
        copy = pltpu.make_async_copy(lhs, rhs.at[:, my_half], local_sem.at[1])
        copy.start()
        copy.wait()

    for d in range(1, npix):
        q = mixed(p, d, npix)
        arrived(terms_f.at[q], f_recv.at[q])
    proj[...] = functools.reduce(lambda x, y: x + y, [terms_f[q] for q in range(npix)])
    for d in range(1, nact):
        b = lax.rem(a + d, nact)
        arrived(terms_s.at[b], p_recv.at[b])
    pred[...] = functools.reduce(lambda x, y: x + y, [terms_s[b] for b in range(nact)])
    for q in range(npix):
        for k in range(chunks):
            ref = rhs.at[at_rows(q, k), other_half]
            arrived(ref, t_recv.at[q, k])
    for cond, make in pending:

        @pl.when(cond)
        def _():
            make().wait_send()


def gathered(npix, nact, jacobian, dark_field, update, pixel_mask, act_mask):
    rows, cols = jacobian.shape
    chunks, via_line = 4, 3
    ngrp = nact // 2
    pm = pixel_mask.astype(F32)
    am = act_mask.astype(F32)
    col = jnp.stack([pm, pm * dark_field], axis=1)
    row = jnp.stack([am, am * update], axis=0)
    n_sends = 0
    n_sends += chunks * (2 + npix - 1 + 1) + 2 * via_line
    n_sends += npix - 1 + nact - 1
    n_sends += chunks * (npix - 1) + 2 * (chunks - via_line) * (npix - 1)
    n_sends += via_line * (ngrp - 1) * 2 * 2
    n_sends += chunks * npix + 2 * (chunks + (chunks - via_line) * (npix - 1))
    vmem = pl.BlockSpec(memory_space=pltpu.VMEM)
    hbm = pl.BlockSpec(memory_space=pl.ANY)
    dma = pltpu.SemaphoreType.DMA
    return pl.pallas_call(
        functools.partial(gather_kernel, npix, ngrp, chunks, via_line),
        out_shape=(
            jax.ShapeDtypeStruct((npix * rows, cols), BF16),
            jax.ShapeDtypeStruct((npix * rows, 2 * cols), BF16),
            jax.ShapeDtypeStruct((1, cols), F32),
            jax.ShapeDtypeStruct((1, rows), F32),
        ),
        in_specs=[vmem] * 3,
        out_specs=(hbm, hbm, vmem, vmem),
        scratch_shapes=[
            pltpu.VMEM((rows, cols), BF16),
            pltpu.VMEM((ngrp, via_line, rows // chunks, cols), BF16),
            pltpu.VMEM((npix, 1, cols), F32),
            pltpu.VMEM((nact, 1, rows), F32),
            dma((npix, chunks)),
            dma((npix, chunks)),
            dma((npix, chunks)),
            dma((ngrp, via_line)),
            dma((npix,)),
            dma((nact,)),
            dma((n_sends,)),
            dma((2,)),
        ],
        compiler_params=pltpu.CompilerParams(
            collective_id=0, has_side_effects=True, vmem_limit_bytes=40 * 1024 * 1024
        ),
    )(jacobian, col, row)


def local(npix, nact, jacobian, dark_field, update, pixel_mask, act_mask):
    lhs, rhs, projected, predicted = gathered(
        npix, nact, jacobian, dark_field, update, pixel_mask, act_mask
    )
    gram_matrix = lax.dot_general(lhs, rhs, (((0,), (0,)), ((), ())), preferred_element_type=F32)
    return gram_matrix, projected[0], predicted[0]


def solution(mesh):
    npix, nact = mesh.shape["pix"], mesh.shape["act"]
    return jax.shard_map(
        functools.partial(local, npix, nact),
        mesh=mesh,
        in_specs=(P("pix", "act"), P("pix"), P("act"), P("pix"), P("act")),
        out_specs=(P("act", "pix"), P("act"), P("pix")),
        check_vma=False,
    )
```

```python
import functools

import jax
import jax.numpy as jnp
from jax import lax
from jax.experimental import pallas as pl
from jax.experimental.pallas import tpu as pltpu
from jax.sharding import PartitionSpec as P

MESH = pl.DeviceIdType.MESH
F32 = jnp.float32
BF16 = jnp.bfloat16
MIB = 1024 * 1024
FIRST = 18
SECOND = 9


def mixed(index, step, size):
    bit, out = 1, index
    while bit < size:
        if step & bit:
            out = out + bit - 2 * bit * ((index // bit) % 2)
        bit *= 2
    return out


def gather_kernel(
    npix, ngrp, chunks, via_line, early, jac, pmask, field, amask, update, lt, late, gram, proj, pred,
    lhs, first, relay, terms_f, terms_s, l_recv, r_recv, t_recv, s_recv, f_recv, p_recv, sends, local_sem,
):
    rows, cols = jac.shape
    wide = cols // chunks
    lanes = wide // 128
    p = lax.axis_index("pix")
    a = lax.axis_index("act")
    z = a // 2
    c = a % 2
    root = p == z
    here = z >= 0
    nact = 2 * ngrp

    barrier = pltpu.get_barrier_semaphore()
    for d in range(1, npix):
        pl.semaphore_signal(barrier, inc=1, device_id={"pix": mixed(p, d, npix), "act": a}, device_id_type=MESH)
    for d in range(1, nact):
        pl.semaphore_signal(barrier, inc=1, device_id={"pix": p, "act": lax.rem(a + d, nact)}, device_id_type=MESH)

    def rows_of(q):
        return pl.ds(pl.multiple_of(q * rows, rows), rows)

    def down_rows(v):
        return jnp.broadcast_to(v, (128, rows)).T

    pm = pmask[...].astype(F32)
    kept = down_rows(pm)
    weighted = down_rows(pm * field[...])

    def mask_step(k, carry):
        for i in range(lanes):
            at = pl.ds(pl.multiple_of((k * lanes + i) * 128, 128), 128)
            keep = kept * amask[:, at].astype(F32) > 0
            masked = jnp.where(keep, jac[:, at].astype(F32), 0.0)
            lhs[k, rows_of(p), i * 128:(i + 1) * 128] = masked.astype(BF16)
        return carry

    lax.fori_loop(0, chunks, mask_step, 0)
    pl.semaphore_wait(barrier, npix - 1 + nact - 1)

    pending = []

    def send(cond, src, dst, rsem, pix, act):
        ssem = sends.at[len(pending)]

        def make():
            return pltpu.make_async_remote_copy(
                src_ref=src, dst_ref=dst, send_sem=ssem, recv_sem=rsem,
                device_id={"pix": pix, "act": act}, device_id_type=MESH,
            )

        @pl.when(cond)
        def _():
            make().start()

        pending.append((cond, make))

    def arrived(ref, sem):
        pltpu.make_async_copy(ref, ref, sem).wait()

    my_half = pl.ds(pl.multiple_of(c * wide, 128), wide)
    other_half = pl.ds(pl.multiple_of((1 - c) * wide, 128), wide)

    def rhs(k):
        return first.at[k] if k < early else late.at[k - early]

    def l_ref(q, k):
        return lhs.at[k, rows_of(q), :]

    def r_ref(q, k):
        return rhs(k).at[rows_of(q), my_half]

    def own(k):
        return l_ref(p, k)

    def turn(q, k):
        lt[k, :, pl.ds(pl.multiple_of(q * rows, rows), rows)] = lhs[k, rows_of(q), :].T

    up = z + 1 < ngrp
    down = z > 0

    def along_line(cond, src, q, k):
        send(cond & up & (z >= p), src, r_ref(q, k), r_recv.at[q, k], p, a + 2)
        send(cond & down & (z <= p), src, r_ref(q, k), r_recv.at[q, k], p, a - 2)

    def to_twin(cond, src, q, k):
        send(cond, src, r_ref(q, k), t_recv.at[q, k], p, 2 * z + 1 - c)

    for k in range(chunks):
        along_line(root, own(k), p, k)
        if k < via_line:
            send(jnp.logical_not(root) & up, own(k), relay.at[z, k], s_recv.at[z, k], p, a + 2)
            send(jnp.logical_not(root) & down, own(k), relay.at[z, k], s_recv.at[z, k], p, a - 2)
        for d in range(1, npix):
            send(here, own(k), l_ref(p, k), l_recv.at[p, k], mixed(p, d, npix), a)
    for k in range(chunks):
        to_twin(root, own(k), p, k)

    def term_step(k, acc):
        for i in range(lanes):
            at = pl.ds(pl.multiple_of((k * lanes + i) * 128, 128), 128)
            tile = lhs[k, rows_of(p), i * 128:(i + 1) * 128].astype(F32)
            terms_f[p, :, at] = jnp.sum(tile * weighted, axis=0, keepdims=True)
            acc = acc + tile * (amask[:, at].astype(F32) * update[:, at])
        return acc

    acc = lax.fori_loop(0, chunks, term_step, jnp.zeros((rows, 128), F32))
    terms_s[a] = jnp.sum(acc.T, axis=0, keepdims=True)
    for d in range(1, npix):
        send(here, terms_f.at[p], terms_f.at[p], f_recv.at[p], mixed(p, d, npix), a)
    for d in range(1, nact):
        send(here, terms_s.at[a], terms_s.at[a], p_recv.at[a], p, lax.rem(a + d, nact))

    for k in range(chunks):
        turn(p, k)

    events = []

    def on_l(d, k):
        def run():
            q = mixed(p, d, npix)
            arrived(l_ref(q, k), l_recv.at[q, k])
            if k >= via_line:
                along_line(root, l_ref(q, k), q, k)
            to_twin(root, l_ref(q, k), q, k)
            turn(q, k)

        return run

    def on_s(dist, sign, k):
        def run():
            g = z - sign * dist
            there = (g >= 0) & (g < ngrp) & (g != p)
            slot = jnp.clip(g, 0, ngrp - 1)

            @pl.when(there)
            def _():
                arrived(relay.at[slot, k], s_recv.at[slot, k])

            if sign > 0:
                send(there & up, relay.at[slot, k], relay.at[slot, k], s_recv.at[slot, k], p, a + 2)
            else:
                send(there & down, relay.at[slot, k], relay.at[slot, k], s_recv.at[slot, k], p, a - 2)
            send(there, relay.at[slot, k], r_ref(p, k), r_recv.at[p, k], slot, a)

        return run

    def on_r(d, k):
        def run():
            q = mixed(p, d, npix)
            other = jnp.logical_not(root)

            @pl.when(other)
            def _():
                arrived(r_ref(q, k), r_recv.at[q, k])

            if d == 0 or k >= via_line:
                along_line(other, r_ref(q, k), q, k)
            to_twin(other, r_ref(q, k), q, k)

        return run

    def on_root():
        @pl.when(root)
        def _():
            copies = [
                pltpu.make_async_copy(lhs.at[k], rhs(k).at[:, my_half], local_sem.at[k])
                for k in range(chunks)
            ]
            for copy in copies:
                copy.start()
            for copy in copies:
                copy.wait()

    def on_twin(k):
        def run():
            for q in range(npix):
                arrived(rhs(k).at[rows_of(q), other_half], t_recv.at[q, k])

        return run

    def on_product(k):
        def run():
            def step(j, carry):
                gram[k, j] = jnp.dot(lt[j], first[k], preferred_element_type=F32)
                return carry

            lax.fori_loop(0, chunks, step, 0)

        return run

    unit = 4.0 / chunks
    for k in range(chunks):
        for d in range(1, npix):
            events.append((12 * unit * (k + 1) + 0.01 * d, on_l(d, k)))
        if k < via_line:
            for dist in range(1, ngrp):
                for sign in (1, -1):
                    events.append((6 * unit * (k + 1) + 18 * (dist - 1), on_s(dist, sign, k)))
        for d in range(npix):
            if d == 0:
                when = 6 * unit * (k + 1) + 12
            elif k >= via_line:
                when = 12 * unit * (k + 1) + 18
            else:
                when = 100 + k
            events.append((when, on_r(d, k)))
        if k < early:
            events.append((100.4 + k, on_twin(k)))
            events.append((100.5 + k, on_product(k)))
        else:
            events.append((200 + k, on_twin(k)))
    events.append((99, on_root))
    events.sort(key=lambda e: e[0])
    for _, run in events:
        run()

    for d in range(1, npix):
        q = mixed(p, d, npix)
        arrived(terms_f.at[q], f_recv.at[q])
    proj[...] = functools.reduce(lambda x, y: x + y, [terms_f[q] for q in range(npix)])
    for d in range(1, nact):
        b = lax.rem(a + d, nact)
        arrived(terms_s.at[b], p_recv.at[b])
    pred[...] = functools.reduce(lambda x, y: x + y, [terms_s[b] for b in range(nact)])
    for cond, make in pending:

        @pl.when(cond)
        def _():
            make().wait_send()


def rest_kernel(early, lt, rhs, done, gram, product, sems):
    chunks, wide, _ = lt.shape
    cols = chunks * wide
    copies = []
    for k in range(early):
        for h in range(2):
            for j in range(chunks):
                copy = pltpu.make_async_copy(
                    done.at[k, j, :, h * wide:(h + 1) * wide],
                    gram.at[j * wide:(j + 1) * wide, h * cols + k * wide:h * cols + (k + 1) * wide],
                    sems.at[k, h, j],
                )
                copy.start()
                copies.append(copy)
    held = []
    for k in range(early, chunks):
        for j in range(chunks):
            slot = len(held) % product.shape[0]
            if len(held) >= product.shape[0]:
                for copy in held[len(held) - product.shape[0]]:
                    copy.wait()
            product[slot] = jnp.dot(lt[j], rhs[k - early], preferred_element_type=F32)
            held.append([])
            for h in range(2):
                copy = pltpu.make_async_copy(
                    product.at[slot, :, h * wide:(h + 1) * wide],
                    gram.at[j * wide:(j + 1) * wide, h * cols + k * wide:h * cols + (k + 1) * wide],
                    sems.at[k, h, j],
                )
                copy.start()
                held[-1].append(copy)
    for pair in held[-product.shape[0]:]:
        copies += pair
    for copy in copies:
        copy.wait()


def local(npix, nact, jacobian, dark_field, update, pixel_mask, act_mask):
    rows, cols = jacobian.shape
    chunks = next(n for n in (6, 3, 2, 1) if cols % (128 * n) == 0)
    via_line, early = max(1, chunks * 5 // 6), chunks * 2 // 3
    wide = cols // chunks
    ngrp = nact // 2
    n_sends = 0
    n_sends += chunks * (2 + npix - 1 + 1) + 2 * via_line
    n_sends += npix - 1 + nact - 1
    n_sends += chunks * (npix - 1) + 2 * (chunks - via_line) * (npix - 1)
    n_sends += via_line * (ngrp - 1) * 2 * 2
    n_sends += chunks * npix + 2 * (chunks + (chunks - via_line) * (npix - 1))
    vmem = pl.BlockSpec(memory_space=pltpu.VMEM)
    hbm = pl.BlockSpec(memory_space=pl.ANY)
    dma = pltpu.SemaphoreType.DMA
    lt, rhs, done, projected, predicted = pl.pallas_call(
        functools.partial(gather_kernel, npix, ngrp, chunks, via_line, early),
        out_shape=(
            jax.ShapeDtypeStruct((chunks, wide, npix * rows), BF16),
            jax.ShapeDtypeStruct((chunks - early, npix * rows, 2 * wide), BF16),
            jax.ShapeDtypeStruct((early, chunks, wide, 2 * wide), F32),
            jax.ShapeDtypeStruct((1, cols), F32),
            jax.ShapeDtypeStruct((1, rows), F32),
        ),
        in_specs=[vmem] * 5,
        out_specs=(vmem,) * 5,
        scratch_shapes=[
            pltpu.VMEM((chunks, npix * rows, wide), BF16),
            pltpu.VMEM((early, npix * rows, 2 * wide), BF16),
            pltpu.VMEM((ngrp, via_line, rows, wide), BF16),
            pltpu.VMEM((npix, 1, cols), F32),
            pltpu.VMEM((nact, 1, rows), F32),
            dma((npix, chunks)),
            dma((npix, chunks)),
            dma((npix, chunks)),
            dma((ngrp, via_line)),
            dma((npix,)),
            dma((nact,)),
            dma((n_sends,)),
            dma((chunks,)),
        ],
        compiler_params=pltpu.CompilerParams(
            collective_id=0, has_side_effects=True, vmem_limit_bytes=FIRST * MIB
        ),
    )(jacobian, pixel_mask[None], dark_field[None], act_mask[None], update[None])
    gram_matrix = pl.pallas_call(
        functools.partial(rest_kernel, early),
        out_shape=jax.ShapeDtypeStruct((cols, 2 * cols), F32),
        in_specs=[vmem, vmem, hbm],
        out_specs=hbm,
        scratch_shapes=[
            pltpu.VMEM((4, wide, 2 * wide), F32),
            dma((chunks, 2, chunks)),
        ],
        compiler_params=pltpu.CompilerParams(vmem_limit_bytes=SECOND * MIB),
    )(lt, rhs, done)
    return gram_matrix, projected[0], predicted[0]


def solution(mesh):
    npix, nact = mesh.shape["pix"], mesh.shape["act"]
    return jax.shard_map(
        functools.partial(local, npix, nact),
        mesh=mesh,
        in_specs=(P("pix", "act"), P("pix"), P("act"), P("pix"), P("act")),
        out_specs=(P("act", "pix"), P("act"), P("pix")),
        check_vma=False,
    )
```

```python
import functools

import jax
import jax.numpy as jnp
from jax import lax
from jax.experimental import pallas as pl
from jax.experimental.pallas import tpu as pltpu
from jax.sharding import PartitionSpec as P

MESH = pl.DeviceIdType.MESH
F32 = jnp.float32
BF16 = jnp.bfloat16
MIB = 1024 * 1024
FIRST = 18
SECOND = 9


def mixed(index, step, size):
    bit, out = 1, index
    while bit < size:
        if step & bit:
            out = out + bit - 2 * bit * ((index // bit) % 2)
        bit *= 2
    return out


def gather_kernel(
    npix, ngrp, chunks, via_line, early, jac, pmask, field, amask, update, lt, late, gram, proj, pred,
    lhs, first, relay, terms_f, terms_s, l_recv, r_recv, t_recv, s_recv, f_recv, p_recv, sends, local_sem,
):
    rows, cols = jac.shape
    wide = cols // chunks
    lanes = wide // 128
    p = lax.axis_index("pix")
    a = lax.axis_index("act")
    z = a // 2
    c = a % 2
    root = p == z
    here = z >= 0
    nact = 2 * ngrp

    barrier = pltpu.get_barrier_semaphore()
    for d in range(1, npix):
        pl.semaphore_signal(barrier, inc=1, device_id={"pix": mixed(p, d, npix), "act": a}, device_id_type=MESH)
    for d in range(1, nact):
        pl.semaphore_signal(barrier, inc=1, device_id={"pix": p, "act": lax.rem(a + d, nact)}, device_id_type=MESH)

    def rows_of(q):
        return pl.ds(pl.multiple_of(q * rows, rows), rows)

    def down_rows(v):
        return jnp.broadcast_to(v, (128, rows)).T

    pm = pmask[...].astype(F32)
    kept = down_rows(pm)
    weighted = down_rows(pm * field[...])

    def mask_step(k, carry):
        for i in range(lanes):
            at = pl.ds(pl.multiple_of((k * lanes + i) * 128, 128), 128)
            keep = kept * amask[:, at].astype(F32) > 0
            masked = jnp.where(keep, jac[:, at].astype(F32), 0.0)
            lhs[k, rows_of(p), i * 128:(i + 1) * 128] = masked.astype(BF16)
        return carry

    lax.fori_loop(0, chunks, mask_step, 0)
    pl.semaphore_wait(barrier, npix - 1 + nact - 1)

    pending = []

    def send(cond, src, dst, rsem, pix, act):
        ssem = sends.at[len(pending)]

        def make():
            return pltpu.make_async_remote_copy(
                src_ref=src, dst_ref=dst, send_sem=ssem, recv_sem=rsem,
                device_id={"pix": pix, "act": act}, device_id_type=MESH,
            )

        @pl.when(cond)
        def _():
            make().start()

        pending.append((cond, make))

    def arrived(ref, sem):
        pltpu.make_async_copy(ref, ref, sem).wait()

    my_half = pl.ds(pl.multiple_of(c * wide, 128), wide)
    other_half = pl.ds(pl.multiple_of((1 - c) * wide, 128), wide)

    def rhs(k):
        return first.at[k] if k < early else late.at[k - early]

    def l_ref(q, k):
        return lhs.at[k, rows_of(q), :]

    def r_ref(q, k):
        return rhs(k).at[rows_of(q), my_half]

    def own(k):
        return l_ref(p, k)

    def turn(q, k):
        lt[k, :, pl.ds(pl.multiple_of(q * rows, rows), rows)] = lhs[k, rows_of(q), :].T

    up = z + 1 < ngrp
    down = z > 0

    def along_line(cond, src, q, k):
        send(cond & up & (z >= p), src, r_ref(q, k), r_recv.at[q, k], p, a + 2)
        send(cond & down & (z <= p), src, r_ref(q, k), r_recv.at[q, k], p, a - 2)

    def to_twin(cond, src, q, k):
        send(cond, src, r_ref(q, k), t_recv.at[q, k], p, 2 * z + 1 - c)

    for k in range(chunks):
        along_line(root, own(k), p, k)
        if k < via_line:
            send(jnp.logical_not(root) & up, own(k), relay.at[z, k], s_recv.at[z, k], p, a + 2)
            send(jnp.logical_not(root) & down, own(k), relay.at[z, k], s_recv.at[z, k], p, a - 2)
        for d in range(1, npix):
            send(here, own(k), l_ref(p, k), l_recv.at[p, k], mixed(p, d, npix), a)
    for k in range(chunks):
        to_twin(root, own(k), p, k)

    def term_step(k, acc):
        for i in range(lanes):
            at = pl.ds(pl.multiple_of((k * lanes + i) * 128, 128), 128)
            tile = lhs[k, rows_of(p), i * 128:(i + 1) * 128].astype(F32)
            terms_f[p, :, at] = jnp.sum(tile * weighted, axis=0, keepdims=True)
            acc = acc + tile * (amask[:, at].astype(F32) * update[:, at])
        return acc

    acc = lax.fori_loop(0, chunks, term_step, jnp.zeros((rows, 128), F32))
    terms_s[a] = jnp.sum(acc.T, axis=0, keepdims=True)
    for d in range(1, npix):
        send(here, terms_f.at[p], terms_f.at[p], f_recv.at[p], mixed(p, d, npix), a)
    for d in range(1, nact):
        send(here, terms_s.at[a], terms_s.at[a], p_recv.at[a], p, lax.rem(a + d, nact))

    for k in range(chunks):
        turn(p, k)

    events = []

    def on_l(d, k):
        def run():
            q = mixed(p, d, npix)
            arrived(l_ref(q, k), l_recv.at[q, k])
            if k >= via_line:
                along_line(root, l_ref(q, k), q, k)
            to_twin(root, l_ref(q, k), q, k)
            turn(q, k)

        return run

    def on_s(dist, sign, k):
        def run():
            g = z - sign * dist
            there = (g >= 0) & (g < ngrp) & (g != p)
            slot = jnp.clip(g, 0, ngrp - 1)

            @pl.when(there)
            def _():
                arrived(relay.at[slot, k], s_recv.at[slot, k])

            if sign > 0:
                send(there & up, relay.at[slot, k], relay.at[slot, k], s_recv.at[slot, k], p, a + 2)
            else:
                send(there & down, relay.at[slot, k], relay.at[slot, k], s_recv.at[slot, k], p, a - 2)
            send(there, relay.at[slot, k], r_ref(p, k), r_recv.at[p, k], slot, a)

        return run

    def on_r(d, k):
        def run():
            q = mixed(p, d, npix)
            other = jnp.logical_not(root)

            @pl.when(other)
            def _():
                arrived(r_ref(q, k), r_recv.at[q, k])

            if d == 0 or k >= via_line:
                along_line(other, r_ref(q, k), q, k)
            to_twin(other, r_ref(q, k), q, k)

        return run

    def on_root():
        @pl.when(root)
        def _():
            copies = [
                pltpu.make_async_copy(lhs.at[k], rhs(k).at[:, my_half], local_sem.at[k])
                for k in range(chunks)
            ]
            for copy in copies:
                copy.start()
            for copy in copies:
                copy.wait()

    def on_twin(k):
        def run():
            for q in range(npix):
                arrived(rhs(k).at[rows_of(q), other_half], t_recv.at[q, k])

        return run

    def on_product(k, j):
        def run():
            gram[k, j] = jnp.dot(lt[j], first[k], preferred_element_type=F32)

        return run

    unit = 4.0 / chunks
    for k in range(chunks):
        for d in range(1, npix):
            events.append((12 * unit * (k + 1) + 0.01 * d, on_l(d, k)))
        if k < via_line:
            for dist in range(1, ngrp):
                for sign in (1, -1):
                    events.append((6 * unit * (k + 1) + 18 * (dist - 1), on_s(dist, sign, k)))
        for d in range(npix):
            if d == 0:
                when = 6 * unit * (k + 1) + 12
            elif k >= via_line:
                when = 12 * unit * (k + 1) + 18
            else:
                when = 67 + 4 * unit * k
            events.append((when, on_r(d, k)))
        if k < early:
            events.append((69 + 4 * unit * k, on_twin(k)))
            for j in range(chunks):
                events.append((69.5 + 4 * unit * k + j * 0.5, on_product(k, j)))
        else:
            events.append((200 + k, on_twin(k)))
    events.append((49, on_root))
    events.sort(key=lambda e: e[0])
    for _, run in events:
        run()

    for d in range(1, npix):
        q = mixed(p, d, npix)
        arrived(terms_f.at[q], f_recv.at[q])
    proj[...] = functools.reduce(lambda x, y: x + y, [terms_f[q] for q in range(npix)])
    for d in range(1, nact):
        b = lax.rem(a + d, nact)
        arrived(terms_s.at[b], p_recv.at[b])
    pred[...] = functools.reduce(lambda x, y: x + y, [terms_s[b] for b in range(nact)])
    for cond, make in pending:

        @pl.when(cond)
        def _():
            make().wait_send()


def rest_kernel(early, lt, rhs, done, gram, product, sems):
    chunks, wide, _ = lt.shape
    cols = chunks * wide
    copies = []
    for k in range(early):
        for h in range(2):
            for j in range(chunks):
                copy = pltpu.make_async_copy(
                    done.at[k, j, :, h * wide:(h + 1) * wide],
                    gram.at[j * wide:(j + 1) * wide, h * cols + k * wide:h * cols + (k + 1) * wide],
                    sems.at[k, h, j],
                )
                copy.start()
                copies.append(copy)
    held = []
    for k in range(early, chunks):
        for j in range(chunks):
            slot = len(held) % product.shape[0]
            if len(held) >= product.shape[0]:
                for copy in held[len(held) - product.shape[0]]:
                    copy.wait()
            product[slot] = jnp.dot(lt[j], rhs[k - early], preferred_element_type=F32)
            held.append([])
            for h in range(2):
                copy = pltpu.make_async_copy(
                    product.at[slot, :, h * wide:(h + 1) * wide],
                    gram.at[j * wide:(j + 1) * wide, h * cols + k * wide:h * cols + (k + 1) * wide],
                    sems.at[k, h, j],
                )
                copy.start()
                held[-1].append(copy)
    for pair in held[-product.shape[0]:]:
        copies += pair
    for copy in copies:
        copy.wait()


def local(npix, nact, jacobian, dark_field, update, pixel_mask, act_mask):
    rows, cols = jacobian.shape
    chunks = next(n for n in (6, 3, 2, 1) if cols % (128 * n) == 0)
    via_line, early = max(1, chunks * 5 // 6), max(1, chunks // 3)
    wide = cols // chunks
    ngrp = nact // 2
    n_sends = 0
    n_sends += chunks * (2 + npix - 1 + 1) + 2 * via_line
    n_sends += npix - 1 + nact - 1
    n_sends += chunks * (npix - 1) + 2 * (chunks - via_line) * (npix - 1)
    n_sends += via_line * (ngrp - 1) * 2 * 2
    n_sends += chunks * npix + 2 * (chunks + (chunks - via_line) * (npix - 1))
    vmem = pl.BlockSpec(memory_space=pltpu.VMEM)
    hbm = pl.BlockSpec(memory_space=pl.ANY)
    dma = pltpu.SemaphoreType.DMA
    lt, rhs, done, projected, predicted = pl.pallas_call(
        functools.partial(gather_kernel, npix, ngrp, chunks, via_line, early),
        out_shape=(
            jax.ShapeDtypeStruct((chunks, wide, npix * rows), BF16),
            jax.ShapeDtypeStruct((chunks - early, npix * rows, 2 * wide), BF16),
            jax.ShapeDtypeStruct((early, chunks, wide, 2 * wide), F32),
            jax.ShapeDtypeStruct((1, cols), F32),
            jax.ShapeDtypeStruct((1, rows), F32),
        ),
        in_specs=[vmem] * 5,
        out_specs=(vmem,) * 5,
        scratch_shapes=[
            pltpu.VMEM((chunks, npix * rows, wide), BF16),
            pltpu.VMEM((early, npix * rows, 2 * wide), BF16),
            pltpu.VMEM((ngrp, via_line, rows, wide), BF16),
            pltpu.VMEM((npix, 1, cols), F32),
            pltpu.VMEM((nact, 1, rows), F32),
            dma((npix, chunks)),
            dma((npix, chunks)),
            dma((npix, chunks)),
            dma((ngrp, via_line)),
            dma((npix,)),
            dma((nact,)),
            dma((n_sends,)),
            dma((chunks,)),
        ],
        compiler_params=pltpu.CompilerParams(
            collective_id=0, has_side_effects=True, vmem_limit_bytes=FIRST * MIB
        ),
    )(jacobian, pixel_mask[None], dark_field[None], act_mask[None], update[None])
    gram_matrix = pl.pallas_call(
        functools.partial(rest_kernel, early),
        out_shape=jax.ShapeDtypeStruct((cols, 2 * cols), F32),
        in_specs=[vmem, vmem, hbm],
        out_specs=hbm,
        scratch_shapes=[
            pltpu.VMEM((4, wide, 2 * wide), F32),
            dma((chunks, 2, chunks)),
        ],
        compiler_params=pltpu.CompilerParams(vmem_limit_bytes=SECOND * MIB),
    )(lt, rhs, done)
    return gram_matrix, projected[0], predicted[0]


def solution(mesh):
    npix, nact = mesh.shape["pix"], mesh.shape["act"]
    return jax.shard_map(
        functools.partial(local, npix, nact),
        mesh=mesh,
        in_specs=(P("pix", "act"), P("pix"), P("act"), P("pix"), P("act")),
        out_specs=(P("act", "pix"), P("act"), P("pix")),
        check_vma=False,
    )
```
